32 devices in a mesh: mem: 2 (over x), space: 16 (over z, y, core).
Axes of the slice: x: 2, y: 2, z: 4, core: 2. Of those that a mesh axis runs over, the one named last changes fastest.
Arguments:
- prior_sample_states: float32 [16, 12, 4096], P('mem', None, 'space'), may hold values from -6 to 6
- depth: float32 [4, 4096], P(None, 'space'), may hold values from 0.5 to 2
- neighbours: int32 [4, 4096], P(None, 'space'), may hold values from 0 to 767, as said below
- obs_element: int32 [16384], P('space'), may hold values from 0 to 255
- obs_count: int32 [16], P('space'), may hold values from 512 to 1024
- obs_values: float32 [16384], P('space'), may hold values from -8 to 8
- obs_error: float32 [16384], P('space'), may hold values from 0.5 to 2
Outputs:
- analysis: float32 [16, 12, 4096], P('mem', None, 'space')
The draws below stay inside these ranges and needn't reach their ends.
Inputs may be any that keep to these rules, and one draw needn't show every extreme that they name: `neighbours`: west and south entries are e + 256 - k and east and north entries e + 256 + k for element e of its block with k from 1 to 256; the first element's west entry and the last element's east entry are at the ends.
All inputs are finite; a program needn't handle non-finite values.
Results may differ from the reference program's by a relative error of at most 0.00015.
Values sent between devices are 32-bit elements; how exact they have to be, the bound alone decides.
A program may use at most 64 MiB of HBM per device.

```python
import math
import jax
import jax.numpy as jnp
from jax import lax

MEMBERS = 16
ELEM_DEV = 256
RIM = 256
BLOCKS = 16
ELEMS = 4096
OBS_DEV = 1024
OBSERV = 16384
STEPS = 1
GN_ITERS = 2


def draw_neighbours(key, part):
    key = jax.random.fold_in(key, 11)
    element = jnp.arange(ELEMS, dtype=jnp.int32) % ELEM_DEV
    reach = jax.random.randint(key, (4, ELEMS), 1, RIM + 1)
    signs = jnp.array([-1, 1, -1, 1], dtype=jnp.int32)[:, None]
    offset = signs * reach
    offset = offset.at[0].set(jnp.where(element == 0, -RIM, offset[0]))
    offset = offset.at[1].set(jnp.where(element == ELEM_DEV - 1, RIM, offset[1]))
    return (element[None, :] + RIM + offset).astype(jnp.int32)


def draw_obs_count(key, part):
    key = jax.random.fold_in(key, 13)
    first, second = jax.random.split(key)
    counts = jax.random.randint(first, (BLOCKS,), OBS_DEV // 2, OBS_DEV + 1)
    order = jax.random.permutation(second, BLOCKS)
    counts = counts.at[order[0]].set(OBS_DEV)
    counts = counts.at[order[1]].set(OBS_DEV // 2)
    return counts.astype(jnp.int32)


def with_ends(values, key, smallest, high):
    dims = values.shape
    index_at = [jax.random.randint(jax.random.fold_in(key, axis), (), 0, dims[axis]) for axis in range(len(dims))]
    values = values.at[tuple(index_at)].set(smallest)
    longest = dims.index(max(dims))
    index_at[longest] = (index_at[longest] + 1) % dims[longest]
    return values.at[tuple(index_at)].set(high)


def steps_of(own_key, extent, pieces, smallest, high):
    gain, own = 1.0, jax.random.fold_in(own_key, 6)
    for dim, shards_of in pieces:
        draws = jnp.exp(jax.random.uniform(jax.random.fold_in(own, dim), (shards_of,), jnp.float32, smallest / len(pieces), high / len(pieces)))
        gain = gain * jnp.repeat(draws, extent[dim] // shards_of).reshape([-1 if axis == dim else 1 for axis in range(len(extent))])
    return gain


def gaussian(rng, shape, scale, bound, shards=(), held_as=jnp.bfloat16):
    drawn = jax.random.normal(rng, shape, jnp.float32) * scale
    if len(shards) > 0:
        drawn = steps_of(rng, shape, shards, -0.22, 0.18) * drawn
    return jnp.clip(drawn, min=-bound, max=bound).astype(held_as)


def setup_inputs(seed: int = 0) -> dict:
    streams_of = jax.random.split(jax.random.key(seed), 8)
    return {
        "prior_sample_states": gaussian(streams_of[0], (MEMBERS, 12, ELEMS), 1.0, 6.0, ((0, 2), (2, 16)), jnp.float32),
        "depth": jnp.clip(jnp.exp(math.log(2.0) - 1.3862944 * jax.random.uniform(streams_of[1], (4, ELEMS), jnp.float32) ** steps_of(streams_of[1], (4, ELEMS), ((1, 16),), -0.2, 0.2)), 0.5, 2.0),
        "neighbours": draw_neighbours(jax.random.fold_in(streams_of[7], 71), 0),
        "obs_element": with_ends(jax.random.randint(streams_of[3], (OBSERV,), 0, ELEM_DEV), jax.random.fold_in(streams_of[3], 1), 0, ELEM_DEV - 1).astype(jnp.int32),
        "obs_count": draw_obs_count(jax.random.fold_in(streams_of[7], 71), 0),
        "obs_values": gaussian(streams_of[5], (OBSERV,), 1.5, 8.0, ((0, 16),), jnp.float32),
        "obs_error": jnp.clip(jnp.exp(math.log(2.0) - 1.3862944 * jax.random.uniform(streams_of[6], (OBSERV,), jnp.float32) ** steps_of(streams_of[6], (OBSERV,), ((0, 16),), -0.2, 0.2)), 0.5, 2.0),
    }


CORIOLIS = 0.5
TIME_STEP = 0.08
SECTION_DECAY = (0.0, -5.0 / 9.0, -153.0 / 128.0)
SECTION_GAIN = (1.0 / 3.0, 15.0 / 16.0, 8.0 / 15.0)
FACE_TABLE = ((slice(0, 2), slice(2, 4), -1.0, 0.0), (slice(2, 4), slice(0, 2), 1.0, 0.0), (slice(0, 4, 2), slice(1, 4, 2), 0.0, -1.0), (slice(1, 4, 2), slice(0, 4, 2), 0.0, 1.0))

def derive_x(values):
    diff = values[..., 2:4, :] - values[..., 0:2, :]
    return jnp.concatenate([diff, diff], axis=-2)

def derive_y(values):
    upper = values[..., 1:2, :] - values[..., 0:1, :]
    lower = values[..., 3:4, :] - values[..., 2:3, :]
    return jnp.concatenate([upper, upper, lower, lower], axis=-2)

def normal_flux(state, depth_part, normal_x, normal_y):
    return jnp.stack([depth_part * (normal_x * state[..., 1, :, :] + normal_y * state[..., 2, :, :]), normal_x * state[..., 0, :, :], normal_y * state[..., 0, :, :]], axis=-3)

def tendency(padded, depth_padded, links, margin):
    width = links.shape[1]
    lead = padded.shape[:-2]
    fields = padded[..., margin:margin + width].reshape(lead + (3, 4, width))
    depth_own = depth_padded[:, margin:margin + width]
    height = fields[..., 0, :, :]
    flow_x = fields[..., 1, :, :]
    flow_y = fields[..., 2, :, :]
    rate_h = -(derive_x(depth_own * flow_x) + derive_y(depth_own * flow_y))
    rate_u = -derive_x(height) + CORIOLIS * flow_y
    rate_v = -derive_y(height) - CORIOLIS * flow_x
    rates = jnp.stack([rate_h, rate_u, rate_v], axis=-3)
    for face, (inner, outer, normal_x, normal_y) in enumerate(FACE_TABLE):
        beyond = jnp.take(padded, links[face], axis=-1).reshape(lead + (3, 4, width))
        depth_beyond = jnp.take(depth_padded, links[face], axis=-1)
        own = fields[..., inner, :]
        far = beyond[..., outer, :]
        depth_in = depth_own[inner]
        depth_out = depth_beyond[outer]
        speed = jnp.sqrt(jnp.maximum(depth_in, depth_out))
        jump = normal_flux(own, depth_in, normal_x, normal_y) - normal_flux(far, depth_out, normal_x, normal_y) + speed * (far - own)
        rates = rates.at[..., inner, :].add(jump)
    return rates.reshape(lead + (12, width))

def observe(values):
    return values[..., 0, :] + values[..., 1, :] ** 2 + values[..., 2, :] ** 2

def solve_step(hessian, vector):
    lower = jnp.linalg.cholesky(hessian)
    middle = lax.linalg.triangular_solve(lower, vector[:, None], left_side=True, lower=True)
    result = lax.linalg.triangular_solve(lower, middle, left_side=True, lower=True, transpose_a=True)
    return (result[:, 0], lower)

def mixing(weights, lower, sample_realizations):
    spread = jnp.sqrt(jnp.float32(sample_realizations - 1))
    eye = jnp.eye(sample_realizations, dtype=jnp.float32)
    inverse_t = lax.linalg.triangular_solve(lower, eye, left_side=True, lower=True, transpose_a=True)
    coef = weights[:, None] / spread + inverse_t
    return 1.0 / sample_realizations + coef - lax.optimization_barrier(jnp.mean(coef, axis=0, keepdims=True))

def reference(prior_sample_states, depth, neighbours, obs_element, obs_count, obs_values, obs_error):
    sample_realizations = prior_sample_states.shape[0]
    cells = prior_sample_states.shape[2]
    offsets = jnp.arange(cells, dtype=jnp.int32) // ELEM_DEV * ELEM_DEV
    links = (neighbours + offsets[None, :]).astype(jnp.int32)
    depth_padded = jnp.pad(depth, ((0, 0), (RIM, RIM)))

    def predict_lone_realization(sample_realization):
        state = sample_realization
        store = jnp.zeros_like(sample_realization)
        for step_index in range(STEPS):
            for section_index in range(3):
                padded = jnp.pad(state, ((0, 0), (RIM, RIM)))
                store = SECTION_DECAY[section_index] * store + TIME_STEP * tendency(padded, depth_padded, links, RIM)
                state = state + SECTION_GAIN[section_index] * store
        return state
    predict_onward = lax.map(predict_lone_realization, prior_sample_states)
    overall_number = obs_values.shape[0]
    slots = jnp.arange(overall_number, dtype=jnp.int32)
    blocks = slots // OBS_DEV
    measurement_sites = (obs_element + blocks * ELEM_DEV).astype(jnp.int32)
    used = (slots % OBS_DEV < obs_count[blocks]).astype(jnp.float32)
    weight = used / obs_error
    probed_readings = jnp.take(predict_onward, measurement_sites, axis=2).reshape(sample_realizations, 3, 4, overall_number)
    means = lax.optimization_barrier(jnp.mean(probed_readings, axis=2))
    zbar = lax.optimization_barrier(jnp.mean(means, axis=0))
    spread_z = (means - zbar) / jnp.sqrt(jnp.float32(sample_realizations - 1))
    weights = jnp.zeros((sample_realizations,), jnp.float32)
    eye = jnp.eye(sample_realizations, dtype=jnp.float32)
    lower = eye
    for iteration in range(GN_ITERS):
        centre = zbar + jnp.einsum('m,mco->co', weights, spread_z, precision=lax.Precision.HIGHEST)
        centre_obs = observe(centre)
        sens = (observe(centre[None] + spread_z) - centre_obs[None]) * weight[None]
        innov = (obs_values - centre_obs) * weight
        hessian = eye + jnp.dot(sens, sens.T, precision=lax.Precision.HIGHEST)
        grad = weights - jnp.dot(sens, innov, precision=lax.Precision.HIGHEST)
        step_vec, lower = solve_step(hessian, grad)
        weights = weights - step_vec
    combination_coefficients = mixing(weights, lower, sample_realizations)
    return jnp.einsum('kj,kqp->jqp', combination_coefficients, predict_onward, precision=lax.Precision.HIGHEST)
```

```python
import functools
import math

import jax
import jax.numpy as jnp
from jax import lax
from jax.experimental import pallas as pl
from jax.experimental.pallas import tpu as pltpu
from jax.sharding import PartitionSpec as P

GN_ITERS = 2
CORIOLIS = 0.5
TIME_STEP = 0.08
SECTION_DECAY = (0.0, -5.0 / 9.0, -153.0 / 128.0)
SECTION_GAIN = (1.0 / 3.0, 15.0 / 16.0, 8.0 / 15.0)
FACES = (
    ((0, 1), (2, 3), -1.0, 0.0, 0),
    ((2, 3), (0, 1), 1.0, 0.0, 1),
    ((0, 2), (1, 3), 0.0, -1.0, 0),
    ((1, 3), (0, 2), 0.0, 1.0, 1),
)
SENT = ((1, 2, 3), (0, 1, 2))
MESH = pl.DeviceIdType.MESH
F32, BF16 = jnp.float32, jnp.bfloat16


def split(x):
    high = x.astype(BF16)
    rest = x - high.astype(F32)
    middle = rest.astype(BF16)
    low = (rest - middle.astype(F32)).astype(BF16)
    return jnp.concatenate([high, middle, low], axis=0)


def pick(x, one_hot):
    rows = x.shape[0]
    y = jnp.dot(split(x), one_hot, preferred_element_type=F32)
    return y[:rows] + y[rows : 2 * rows] + y[2 * rows :]


def kernel(
    nm, ns,
    x_ref, dep_ref, nb_ref, oe_ref, cnt_ref, ov_ref, er_ref,
    out_ref,
    st, store, halo, dhalo, oh, fc, em, parts, sums,
    h_send, h_recv, d_send, d_recv, e_send, e_recv, f_send, f_recv, s_send, s_recv,
):
    mm, me = lax.axis_index("mem"), lax.axis_index("space")
    lm, _, width = x_ref.shape
    members = nm * lm
    space_peers = [(mm, lax.rem(me + d, ns)) for d in range(1, ns)]
    mem_peers = [(lax.rem(mm + d, nm), me) for d in range(1, nm)]

    barrier = pltpu.get_barrier_semaphore()
    for peer in space_peers + mem_peers:
        pl.semaphore_signal(barrier, inc=1, device_id=peer, device_id_type=MESH)

    for n in range(4):
        for f in range(3):
            st[0, n * 3 + f] = x_ref[:, f * 4 + n, :]
    has = (me > 0, me < ns - 1)
    for side in range(2):

        @pl.when(jnp.logical_not(has[side]))
        def _():
            for s in range(3):
                halo[s, side] = jnp.zeros(halo.shape[2:], F32)
            dhalo[side] = jnp.zeros(dhalo.shape[1:], F32)

    pl.semaphore_wait(barrier, len(space_peers) + len(mem_peers))

    def halo_copy(s, side):
        first = SENT[1 - side][0] * 3
        target = (mm, lax.rem(me + (ns - 1 if side == 0 else 1), ns))
        return pltpu.make_async_remote_copy(
            src_ref=st.at[s, pl.ds(first, 9)],
            dst_ref=halo.at[s, 1 - side],
            send_sem=h_send.at[s, 1 - side],
            recv_sem=h_recv.at[s, 1 - side],
            device_id=target,
            device_id_type=MESH,
        )

    def depth_copy(side):
        target = (mm, lax.rem(me + (ns - 1 if side == 0 else 1), ns))
        return pltpu.make_async_remote_copy(
            src_ref=dep_ref,
            dst_ref=dhalo.at[1 - side],
            send_sem=d_send.at[1 - side],
            recv_sem=d_recv.at[1 - side],
            device_id=target,
            device_id_type=MESH,
        )

    def send_halo(s):
        for side in range(2):

            @pl.when(has[side])
            def _():
                halo_copy(s, side).start()

    for side in range(2):

        @pl.when(has[side])
        def _():
            depth_copy(side).start()

    send_halo(0)

    rows = lax.broadcasted_iota(jnp.int32, (width, width), 0)
    for face in range(4):
        side = FACES[face][4]
        link = nb_ref[face : face + 1, :]
        oh[face, 0] = jnp.where(rows + width == link, 1.0, 0.0).astype(BF16)
        oh[face, 1] = jnp.where(rows + 2 * width * side == link, 1.0, 0.0).astype(BF16)

    slots = ov_ref.shape[1]
    slot = lax.broadcasted_iota(jnp.int32, (1, slots), 1)
    weight = jnp.where(slot < cnt_ref[0], 1.0, 0.0) / er_ref[...]
    square = weight * weight
    both = jnp.concatenate(
        [jnp.broadcast_to(square, (8, slots)), jnp.broadcast_to(square * ov_ref[...], (8, slots))],
        axis=0,
    )
    at = jnp.where(
        lax.broadcasted_iota(jnp.int32, (width, slots), 0) == oe_ref[...], 1.0, 0.0
    ).astype(BF16)
    y = lax.dot_general(split(both), at, (((1,), (1,)), ((), ())), preferred_element_type=F32)
    y = y[:16] + y[16:32] + y[32:]
    w2, wo = y[0:1], y[8:9]

    def tall(ref, n):
        return jnp.broadcast_to(ref[n : n + 1, :], (lm, width))

    own_depth = [tall(dep_ref, n) for n in range(4)]
    depth_out, speed = {}, {}

    for s in range(3):
        q = [[st[s, n * 3 + f] for f in range(3)] for n in range(4)]
        near = []
        for face, (_, outer, _, _, side) in enumerate(FACES):
            x = jnp.concatenate([q[n][f] for n in outer for f in range(3)], axis=0)
            near.append(pick(x, oh[face, 0]))
        hu = [own_depth[n] * q[n][1] for n in range(4)]
        hv = [own_depth[n] * q[n][2] for n in range(4)]
        rate = [[None] * 3 for _ in range(4)]
        for n in range(4):
            b, a2 = n % 2, n - n % 2
            rate[n][0] = -((hu[2 + b] - hu[b]) + (hv[a2 + 1] - hv[a2]))
            rate[n][1] = q[b][0] - q[2 + b][0] + CORIOLIS * q[n][2]
            rate[n][2] = q[a2][0] - q[a2 + 1][0] - CORIOLIS * q[n][1]
        if s == 0:
            for side in range(2):

                @pl.when(has[side])
                def _():
                    depth_copy(1 - side).wait_recv()

            for face, (inner, outer, _, _, side) in enumerate(FACES):
                here = jnp.concatenate([own_depth[n] for n in outer], axis=0)
                there = jnp.concatenate([tall(dhalo.at[side], n) for n in outer], axis=0)
                got = pick(here, oh[face, 0]) + pick(there, oh[face, 1])
                for i in range(2):
                    depth_out[face, i] = got[i * lm : (i + 1) * lm]
                    speed[face, i] = jnp.sqrt(
                        jnp.maximum(own_depth[inner[i]], depth_out[face, i])
                    )
        for side in range(2):

            @pl.when(has[side])
            def _():
                halo_copy(s, 1 - side).wait_recv()

        for face, (inner, outer, nx, ny, side) in enumerate(FACES):
            x = jnp.concatenate(
                [halo[s, side, SENT[side].index(n) * 3 + f] for n in outer for f in range(3)],
                axis=0,
            )
            far = near[face] + pick(x, oh[face, 1])
            for i in range(2):
                n = inner[i]
                fh, fu, fv = (far[(i * 3 + f) * lm : (i * 3 + f + 1) * lm] for f in range(3))
                sp, do = speed[face, i], depth_out[face, i]
                if nx:
                    rate[n][0] += nx * (hu[n] - do * fu) + sp * (fh - q[n][0])
                    rate[n][1] += nx * (q[n][0] - fh) + sp * (fu - q[n][1])
                    rate[n][2] += sp * (fv - q[n][2])
                else:
                    rate[n][0] += ny * (hv[n] - do * fv) + sp * (fh - q[n][0])
                    rate[n][1] += sp * (fu - q[n][1])
                    rate[n][2] += ny * (q[n][0] - fh) + sp * (fv - q[n][2])
        for n in range(4):
            for f in range(3):
                change = TIME_STEP * rate[n][f]
                if s:
                    change += SECTION_DECAY[s] * store[n * 3 + f]
                q[n][f] = q[n][f] + SECTION_GAIN[s] * change
                if s < 2:
                    store[n * 3 + f] = change
                    st[s + 1, n * 3 + f] = q[n][f]
                else:
                    fc[mm, n * 3 + f] = q[n][f]
        if s < 2:
            send_halo(s + 1)

    for f in range(3):
        em[mm, f] = 0.25 * ((q[0][f] + q[1][f]) + (q[2][f] + q[3][f]))

    def share(buf, send, recv, d):
        return pltpu.make_async_remote_copy(
            src_ref=buf.at[mm],
            dst_ref=buf.at[mm],
            send_sem=send.at[d],
            recv_sem=recv.at[d],
            device_id=mem_peers[d],
            device_id_type=MESH,
        )

    em_copies = [share(em, e_send, e_recv, d) for d in range(nm - 1)]
    fc_copies = [share(fc, f_send, f_recv, d) for d in range(nm - 1)]
    for copy in em_copies + fc_copies:
        copy.start()
    for copy in em_copies:
        copy.wait_recv()

    root = math.sqrt(members - 1)
    zs = [jnp.concatenate([em[j, f] for j in range(nm)], axis=0) for f in range(3)]
    zbar = [jnp.sum(z, axis=0, keepdims=True) * (1.0 / members) for z in zs]
    spread = [(z - b) * (1.0 / root) for z, b in zip(zs, zbar)]

    lanes = sums.shape[2]
    row = lax.broadcasted_iota(jnp.int32, (members, lanes), 0)
    lane = lax.broadcasted_iota(jnp.int32, (members, lanes), 1)
    eyes = jnp.where((lane == row) | (lane == row + members), 1.0, 0.0)
    w_row = w_col = None
    sum_copies = []
    for it in range(GN_ITERS):
        c = zbar
        if it:
            c = [
                b + jnp.sum(w_col * z, axis=0, keepdims=True) for b, z in zip(zbar, spread)
            ]
        hx = c[0] + c[1] * c[1] + c[2] * c[2]
        sens = (
            spread[0]
            + spread[1] * (2.0 * c[1] + spread[1])
            + spread[2] * (2.0 * c[2] + spread[2])
        )
        right = jnp.concatenate(
            [
                jnp.zeros((members, width), F32),
                sens * w2,
                jnp.broadcast_to(hx * w2 - wo, (8, width)),
                jnp.zeros((lanes - 2 * members - 8, width), F32),
            ],
            axis=0,
        )
        sums[it] = lax.dot_general(
            sens, right, (((1,), (1,)), ((), ())),
            precision=lax.Precision.HIGHEST, preferred_element_type=F32,
        )
        copies = [
            pltpu.make_async_remote_copy(
                src_ref=sums.at[it],
                dst_ref=parts.at[it, d],
                send_sem=s_send.at[it, d],
                recv_sem=s_recv.at[it, d],
                device_id=space_peers[d],
                device_id_type=MESH,
            )
            for d in range(ns - 1)
        ]
        for copy in copies:
            copy.start()
        total = sums[it]
        for d, copy in enumerate(copies):
            copy.wait_recv()
            total = total + parts[it, d]
        sum_copies += copies
        a = total + eyes
        if it:
            a = a + jnp.where(lane == 2 * members, w_col, 0.0)
        for k in range(members):
            pivot = a[k : k + 1, :]
            col = a[:, members + k : members + k + 1]
            inv = lax.rsqrt(a[k : k + 1, members + k : members + k + 1])
            pivot = pivot * inv
            a = jnp.where(row > k, a - (col * inv) * pivot, jnp.where(row == k, pivot, a))
        step = jnp.sum(a[:, 2 * members : 2 * members + 1] * a, axis=0, keepdims=True)
        w_row = -step if it == 0 else w_row - step
        w_col = jnp.sum(jnp.where(lane == row, w_row, 0.0), axis=1, keepdims=True)

    coef = jnp.where(lane < members, a + w_row * (1.0 / root), 0.0)
    mix = coef + 1.0 / members - jnp.sum(coef, axis=1, keepdims=True) * (1.0 / members)
    own = mix[0:lm]
    for j in range(1, nm):
        own = jnp.where(mm == j, mix[j * lm : (j + 1) * lm], own)
    gains = [jnp.broadcast_to(own[:, m : m + 1], (lm, width)) for m in range(members)]
    for copy in fc_copies:
        copy.wait_recv()
    for n in range(4):
        for f in range(3):
            acc = None
            for j in range(nm):
                block = fc[j, n * 3 + f]
                for i in range(lm):
                    term = gains[j * lm + i] * block[i : i + 1, :]
                    acc = term if acc is None else acc + term
            out_ref[:, f * 4 + n, :] = acc

    for side in range(2):

        @pl.when(has[side])
        def _():
            depth_copy(side).wait_send()
            for s in range(3):
                halo_copy(s, side).wait_send()

    for copy in em_copies + fc_copies + sum_copies:
        copy.wait_send()


def solution(mesh):
    nm, ns = mesh.shape["mem"], mesh.shape["space"]

    def body(states, depth, neighbours, obs_element, obs_count, obs_values, obs_error):
        lm, comps, width = states.shape
        slots = obs_values.shape[0]
        members = nm * lm
        lanes = -(-(2 * members + 8) // 128) * 128
        vmem = pl.BlockSpec(memory_space=pltpu.VMEM)
        dma = pltpu.SemaphoreType.DMA
        peers = max(nm - 1, 1)
        return pl.pallas_call(
            functools.partial(kernel, nm, ns),
            out_shape=jax.ShapeDtypeStruct(states.shape, F32),
            in_specs=[vmem] * 4 + [pl.BlockSpec(memory_space=pltpu.SMEM)] + [vmem] * 2,
            out_specs=vmem,
            scratch_shapes=[
                pltpu.VMEM((3, comps, lm, width), F32),
                pltpu.VMEM((comps, lm, width), F32),
                pltpu.VMEM((3, 2, 9, lm, width), F32),
                pltpu.VMEM((2, 4, width), F32),
                pltpu.VMEM((4, 2, width, width), BF16),
                pltpu.VMEM((nm, comps, lm, width), F32),
                pltpu.VMEM((nm, 3, lm, width), F32),
                pltpu.VMEM((GN_ITERS, ns - 1, members, lanes), F32),
                pltpu.VMEM((GN_ITERS, members, lanes), F32),
                dma((3, 2)),
                dma((3, 2)),
                dma((2,)),
                dma((2,)),
                dma((peers,)),
                dma((peers,)),
                dma((peers,)),
                dma((peers,)),
                dma((GN_ITERS, ns - 1)),
                dma((GN_ITERS, ns - 1)),
            ],
            compiler_params=pltpu.CompilerParams(
                collective_id=0, has_side_effects=True, vmem_limit_bytes=40 * 1024 * 1024
            ),
        )(
            states,
            depth,
            neighbours,
            obs_element.reshape(1, slots),
            obs_count,
            obs_values.reshape(1, slots),
            obs_error.reshape(1, slots),
        )

    placed = (
        P("mem", None, "space"),
        P(None, "space"),
        P(None, "space"),
        P("space"),
        P("space"),
        P("space"),
        P("space"),
    )
    return jax.shard_map(
        body, mesh=mesh, in_specs=placed, out_specs=P("mem", None, "space"), check_vma=False
    )
```

```python
import functools
import math

import jax
import jax.numpy as jnp
from jax import lax
from jax.experimental import pallas as pl
from jax.experimental.pallas import tpu as pltpu
from jax.sharding import PartitionSpec as P

GN_ITERS = 2
CORIOLIS = 0.5
TIME_STEP = 0.08
SECTION_DECAY = (0.0, -5.0 / 9.0, -153.0 / 128.0)
SECTION_GAIN = (1.0 / 3.0, 15.0 / 16.0, 8.0 / 15.0)
FACES = (
    ((0, 1), (2, 3), -1.0, 0.0, 0),
    ((2, 3), (0, 1), 1.0, 0.0, 1),
    ((0, 2), (1, 3), 0.0, -1.0, 0),
    ((1, 3), (0, 2), 0.0, 1.0, 1),
)
SENT = ((1, 2, 3), (0, 1, 2))
MESH = pl.DeviceIdType.MESH
F32, BF16 = jnp.float32, jnp.bfloat16


def split(x):
    high = x.astype(BF16)
    rest = x - high.astype(F32)
    middle = rest.astype(BF16)
    low = (rest - middle.astype(F32)).astype(BF16)
    return jnp.concatenate([high, middle, low], axis=0)


def pick(x, one_hot):
    rows = x.shape[0]
    y = jnp.dot(split(x), one_hot, preferred_element_type=F32)
    return y[:rows] + y[rows : 2 * rows] + y[2 * rows :]


def pack(x, packed):
    if not packed:
        return x
    half, lanes = x.shape[0] // 2, x.shape[1]
    lane = lax.broadcasted_iota(jnp.int32, (half, lanes), 1)
    return jnp.where(lane < lanes // 2, x[:half], pltpu.roll(x[half:], lanes // 2, 1))


def unpack(x, packed):
    if not packed:
        return x
    return jnp.concatenate([x, pltpu.roll(x, x.shape[1] // 2, 1)], axis=0)


def kernel(
    nm, ns,
    x_in, dep_in, nb_in, oe_in, cnt_ref, ov_in, er_in,
    out_ref,
    dep_ref, nb_ref, oe_ref, ov_ref, er_ref,
    st, store, halo, dhalo, oh, fc, em, parts, sums,
    l_sem, h_send, h_recv, d_send, d_recv, e_send, e_recv, f_send, f_recv, s_send, s_recv,
):
    mm, me = lax.axis_index("mem"), lax.axis_index("space")
    lm, width = x_in.shape[2:]
    members = nm * lm
    loads = [
        pltpu.make_async_copy(src, dst, l_sem.at[i])
        for i, (src, dst) in enumerate(
            [
                (nb_in, nb_ref), (er_in, er_ref), (oe_in, oe_ref), (ov_in, ov_ref),
                (x_in, st.at[0]), (dep_in, dep_ref),
            ]
        )
    ]
    for load in loads:
        load.start()
    inner = 2 if ns % 2 == 0 else 1
    base = lax.div(me, inner) * inner
    stages = [
        [(mm, base + lax.rem(me - base + d, inner)) for d in range(1, inner)],
        [(mm, lax.rem(me + d * inner, ns)) for d in range(1, ns // inner)],
    ]
    stages = [peers for peers in stages if peers]
    space_peers = sum(stages, []) + [(mm, lax.rem(me + d, ns)) for d in (1, ns - 1)]
    mem_peers = [(lax.rem(mm + d, nm), me) for d in range(1, nm)]

    barrier = pltpu.get_barrier_semaphore()
    for peer in space_peers + mem_peers:
        pl.semaphore_signal(barrier, inc=1, device_id=peer, device_id_type=MESH)

    has = (me > 0, me < ns - 1)
    for side in range(2):

        @pl.when(jnp.logical_not(has[side]))
        def _():
            for s in range(3):
                halo[s, side] = jnp.zeros(halo.shape[2:], F32)
            dhalo[side] = jnp.zeros(dhalo.shape[1:], F32)

    pl.semaphore_wait(barrier, len(space_peers) + len(mem_peers))

    def halo_copy(s, side):
        first = SENT[1 - side][0]
        target = (mm, lax.rem(me + (ns - 1 if side == 0 else 1), ns))
        return pltpu.make_async_remote_copy(
            src_ref=(st.at[s] if s else x_in).at[:, pl.ds(first, 3)],
            dst_ref=halo.at[s, 1 - side],
            send_sem=h_send.at[s, 1 - side],
            recv_sem=h_recv.at[s, 1 - side],
            device_id=target,
            device_id_type=MESH,
        )

    def depth_copy(side):
        target = (mm, lax.rem(me + (ns - 1 if side == 0 else 1), ns))
        return pltpu.make_async_remote_copy(
            src_ref=dep_in,
            dst_ref=dhalo.at[1 - side],
            send_sem=d_send.at[1 - side],
            recv_sem=d_recv.at[1 - side],
            device_id=target,
            device_id_type=MESH,
        )

    def send_halo(s):
        for side in range(2):

            @pl.when(has[side])
            def _():
                halo_copy(s, side).start()

    for side in range(2):

        @pl.when(has[side])
        def _():
            depth_copy(side).start()

    send_halo(0)

    loads[0].wait()
    rows = lax.broadcasted_iota(jnp.int32, (width, width), 0)
    for face in range(4):
        side = FACES[face][4]
        link = nb_ref[face : face + 1, :]
        oh[face, 0] = jnp.where(rows + width == link, 1.0, 0.0).astype(BF16)
        oh[face, 1] = jnp.where(rows + 2 * width * side == link, 1.0, 0.0).astype(BF16)

    for load in loads[1:4]:
        load.wait()
    slots = ov_ref.shape[1]
    slot = lax.broadcasted_iota(jnp.int32, (1, slots), 1)
    weight = jnp.where(slot < cnt_ref[0], 1.0, 0.0) / er_ref[...]
    square = weight * weight
    both = jnp.concatenate(
        [jnp.broadcast_to(square, (8, slots)), jnp.broadcast_to(square * ov_ref[...], (8, slots))],
        axis=0,
    )
    at = jnp.where(
        lax.broadcasted_iota(jnp.int32, (width, slots), 0) == oe_ref[...], 1.0, 0.0
    ).astype(BF16)
    y = lax.dot_general(split(both), at, (((1,), (1,)), ((), ())), preferred_element_type=F32)
    y = y[:16] + y[16:32] + y[32:]
    w2, wo = y[0:1], y[8:9]

    def tall(ref, n):
        return jnp.broadcast_to(ref[n : n + 1, :], (lm, width))

    for load in loads[4:]:
        load.wait()
    own_depth = [tall(dep_ref, n) for n in range(4)]
    depth_out, speed = {}, {}

    for s in range(3):
        q = [[st[s, f, n] for f in range(3)] for n in range(4)]
        near = []
        for face, (_, outer, _, _, side) in enumerate(FACES):
            x = jnp.concatenate([q[n][f] for n in outer for f in range(3)], axis=0)
            near.append(pick(x, oh[face, 0]))
        hu = [own_depth[n] * q[n][1] for n in range(4)]
        hv = [own_depth[n] * q[n][2] for n in range(4)]
        rate = [[None] * 3 for _ in range(4)]
        for n in range(4):
            b, a2 = n % 2, n - n % 2
            rate[n][0] = -((hu[2 + b] - hu[b]) + (hv[a2 + 1] - hv[a2]))
            rate[n][1] = q[b][0] - q[2 + b][0] + CORIOLIS * q[n][2]
            rate[n][2] = q[a2][0] - q[a2 + 1][0] - CORIOLIS * q[n][1]
        if s == 0:
            for side in range(2):

                @pl.when(has[side])
                def _():
                    depth_copy(1 - side).wait_recv()

            for face, (inner, outer, _, _, side) in enumerate(FACES):
                here = jnp.concatenate([own_depth[n] for n in outer], axis=0)
                there = jnp.concatenate([tall(dhalo.at[side], n) for n in outer], axis=0)
                got = pick(here, oh[face, 0]) + pick(there, oh[face, 1])
                for i in range(2):
                    depth_out[face, i] = got[i * lm : (i + 1) * lm]
                    speed[face, i] = jnp.sqrt(
                        jnp.maximum(own_depth[inner[i]], depth_out[face, i])
                    )
        for side in range(2):

            @pl.when(has[side])
            def _():
                halo_copy(s, 1 - side).wait_recv()

        for face, (inner, outer, nx, ny, side) in enumerate(FACES):
            x = jnp.concatenate(
                [halo[s, side, f, SENT[side].index(n)] for n in outer for f in range(3)],
                axis=0,
            )
            far = near[face] + pick(x, oh[face, 1])
            for i in range(2):
                n = inner[i]
                fh, fu, fv = (far[(i * 3 + f) * lm : (i * 3 + f + 1) * lm] for f in range(3))
                sp, do = speed[face, i], depth_out[face, i]
                if nx:
                    rate[n][0] += nx * (hu[n] - do * fu) + sp * (fh - q[n][0])
                    rate[n][1] += nx * (q[n][0] - fh) + sp * (fu - q[n][1])
                    rate[n][2] += sp * (fv - q[n][2])
                else:
                    rate[n][0] += ny * (hv[n] - do * fv) + sp * (fh - q[n][0])
                    rate[n][1] += sp * (fu - q[n][1])
                    rate[n][2] += ny * (q[n][0] - fh) + sp * (fv - q[n][2])
        for n in range(4):
            for f in range(3):
                change = TIME_STEP * rate[n][f]
                if s:
                    change += SECTION_DECAY[s] * store[f, n]
                q[n][f] = q[n][f] + SECTION_GAIN[s] * change
                if s < 2:
                    store[f, n] = change
                    st[s + 1, f, n] = q[n][f]
                else:
                    fc[mm, f, n] = q[n][f]
        if s < 2:
            send_halo(s + 1)

    for f in range(3):
        em[mm, f] = 0.25 * ((q[0][f] + q[1][f]) + (q[2][f] + q[3][f]))

    def share(buf, send, recv, d):
        return pltpu.make_async_remote_copy(
            src_ref=buf.at[mm],
            dst_ref=buf.at[mm],
            send_sem=send.at[d],
            recv_sem=recv.at[d],
            device_id=mem_peers[d],
            device_id_type=MESH,
        )

    em_copies = [share(em, e_send, e_recv, d) for d in range(nm - 1)]
    fc_copies = [share(fc, f_send, f_recv, d) for d in range(nm - 1)]
    for copy in em_copies + fc_copies:
        copy.start()
    for copy in em_copies:
        copy.wait_recv()

    root = math.sqrt(members - 1)
    zs = [jnp.concatenate([em[j, f] for j in range(nm)], axis=0) for f in range(3)]
    zbar = [jnp.sum(z, axis=0, keepdims=True) * (1.0 / members) for z in zs]
    spread = [(z - b) * (1.0 / root) for z, b in zip(zs, zbar)]

    lanes = sums.shape[3]
    packed = sums.shape[2] < members
    row = lax.broadcasted_iota(jnp.int32, (members, lanes), 0)
    lane = lax.broadcasted_iota(jnp.int32, (members, lanes), 1)
    eyes = jnp.where((lane == row) | (lane == row + members), 1.0, 0.0)
    w_row = w_col = None
    sum_copies = []
    for it in range(GN_ITERS):
        c = zbar
        if it:
            c = [
                b + jnp.sum(w_col * z, axis=0, keepdims=True) for b, z in zip(zbar, spread)
            ]
        hx = c[0] + c[1] * c[1] + c[2] * c[2]
        sens = (
            spread[0]
            + spread[1] * (2.0 * c[1] + spread[1])
            + spread[2] * (2.0 * c[2] + spread[2])
        )
        right = jnp.concatenate(
            [
                jnp.zeros((members, width), F32),
                sens * w2,
                jnp.broadcast_to(hx * w2 - wo, (8, width)),
                jnp.zeros((lanes - 2 * members - 8, width), F32),
            ],
            axis=0,
        )
        total = lax.dot_general(
            sens, right, (((1,), (1,)), ((), ())),
            precision=lax.Precision.HIGHEST, preferred_element_type=F32,
        )
        total = pack(total, packed)
        slot_at = 0
        for stage, peers in enumerate(stages):
            sums[it, stage] = total
            copies = [
                pltpu.make_async_remote_copy(
                    src_ref=sums.at[it, stage],
                    dst_ref=parts.at[it, slot_at + d],
                    send_sem=s_send.at[it, slot_at + d],
                    recv_sem=s_recv.at[it, slot_at + d],
                    device_id=peer,
                    device_id_type=MESH,
                )
                for d, peer in enumerate(peers)
            ]
            for copy in copies:
                copy.start()
            for d, copy in enumerate(copies):
                copy.wait_recv()
                total = total + parts[it, slot_at + d]
            slot_at += len(peers)
            sum_copies += copies
        total = unpack(total, packed)
        a = total + eyes
        if it:
            a = a + jnp.where(lane == 2 * members, w_col, 0.0)
        for k in range(members):
            pivot = a[k : k + 1, :]
            col = a[:, members + k : members + k + 1]
            inv = lax.rsqrt(a[k : k + 1, members + k : members + k + 1])
            pivot = pivot * inv
            a = jnp.where(row > k, a - (col * inv) * pivot, jnp.where(row == k, pivot, a))
        step = jnp.sum(a[:, 2 * members : 2 * members + 1] * a, axis=0, keepdims=True)
        w_row = -step if it == 0 else w_row - step
        w_col = jnp.sum(jnp.where(lane == row, w_row, 0.0), axis=1, keepdims=True)

    coef = jnp.where(lane < members, a + w_row * (1.0 / root), 0.0)
    mix = coef + 1.0 / members - jnp.sum(coef, axis=1, keepdims=True) * (1.0 / members)
    own = mix[0:lm]
    for j in range(1, nm):
        own = jnp.where(mm == j, mix[j * lm : (j + 1) * lm], own)
    gains = [jnp.broadcast_to(own[:, m : m + 1], (lm, width)) for m in range(members)]
    for copy in fc_copies:
        copy.wait_recv()
    for n in range(4):
        for f in range(3):
            acc = None
            for j in range(nm):
                block = fc[j, f, n]
                for i in range(lm):
                    term = gains[j * lm + i] * block[i : i + 1, :]
                    acc = term if acc is None else acc + term
            out_ref[f * 4 + n] = acc

    for side in range(2):

        @pl.when(has[side])
        def _():
            depth_copy(side).wait_send()
            for s in range(3):
                halo_copy(s, side).wait_send()

    for copy in em_copies + fc_copies + sum_copies:
        copy.wait_send()


def solution(mesh):
    nm, ns = mesh.shape["mem"], mesh.shape["space"]

    def body(states, depth, neighbours, obs_element, obs_count, obs_values, obs_error):
        lm, comps, width = states.shape
        slots = obs_values.shape[0]
        members = nm * lm
        lanes = -(-(2 * members + 8) // 128) * 128
        packed = members % 16 == 0 and 4 * members + 2 <= lanes
        rows = members // 2 if packed else members
        vmem = pl.BlockSpec(memory_space=pltpu.VMEM)
        hbm = pl.BlockSpec(memory_space=pl.ANY)
        dma = pltpu.SemaphoreType.DMA
        peers = max(nm - 1, 1)
        mixed = pl.pallas_call(
            functools.partial(kernel, nm, ns),
            out_shape=jax.ShapeDtypeStruct((comps, lm, width), F32),
            in_specs=[hbm] * 4 + [pl.BlockSpec(memory_space=pltpu.SMEM)] + [hbm] * 2,
            out_specs=vmem,
            scratch_shapes=[
                pltpu.VMEM((4, width), F32),
                pltpu.VMEM((4, width), jnp.int32),
                pltpu.VMEM((1, slots), jnp.int32),
                pltpu.VMEM((1, slots), F32),
                pltpu.VMEM((1, slots), F32),
                pltpu.VMEM((3, 3, 4, lm, width), F32),
                pltpu.VMEM((3, 4, lm, width), F32),
                pltpu.VMEM((3, 2, 3, 3, lm, width), F32),
                pltpu.VMEM((2, 4, width), F32),
                pltpu.VMEM((4, 2, width, width), BF16),
                pltpu.VMEM((nm, 3, 4, lm, width), F32),
                pltpu.VMEM((nm, 3, lm, width), F32),
                pltpu.VMEM((GN_ITERS, ns - 1, rows, lanes), F32),
                pltpu.VMEM((GN_ITERS, 2, rows, lanes), F32),
                dma((6,)),
                dma((3, 2)),
                dma((3, 2)),
                dma((2,)),
                dma((2,)),
                dma((peers,)),
                dma((peers,)),
                dma((peers,)),
                dma((peers,)),
                dma((GN_ITERS, ns - 1)),
                dma((GN_ITERS, ns - 1)),
            ],
            compiler_params=pltpu.CompilerParams(
                collective_id=0, has_side_effects=True, vmem_limit_bytes=56 * 1024 * 1024
            ),
        )(
            states.transpose(1, 0, 2).reshape(3, comps // 3, lm, width),
            depth,
            neighbours,
            obs_element.reshape(1, slots),
            obs_count,
            obs_values.reshape(1, slots),
            obs_error.reshape(1, slots),
        )
        return mixed.transpose(1, 0, 2)

    placed = (
        P("mem", None, "space"),
        P(None, "space"),
        P(None, "space"),
        P("space"),
        P("space"),
        P("space"),
        P("space"),
    )
    return jax.shard_map(
        body, mesh=mesh, in_specs=placed, out_specs=P("mem", None, "space"), check_vma=False
    )
```

```python
import functools
import math

import jax
import jax.numpy as jnp
from jax import lax
from jax.experimental import pallas as pl
from jax.experimental.pallas import tpu as pltpu
from jax.sharding import PartitionSpec as P

GN_ITERS = 2
CORIOLIS = 0.5
TIME_STEP = 0.08
SECTION_DECAY = (0.0, -5.0 / 9.0, -153.0 / 128.0)
SECTION_GAIN = (1.0 / 3.0, 15.0 / 16.0, 8.0 / 15.0)
FACES = (
    ((0, 1), (2, 3), -1.0, 0.0, 0),
    ((2, 3), (0, 1), 1.0, 0.0, 1),
    ((0, 2), (1, 3), 0.0, -1.0, 0),
    ((1, 3), (0, 2), 0.0, 1.0, 1),
)
SENT = ((1, 2, 3), (0, 1, 2))
MESH = pl.DeviceIdType.MESH
F32, BF16 = jnp.float32, jnp.bfloat16


def split(x):
    high = x.astype(BF16)
    rest = x - high.astype(F32)
    middle = rest.astype(BF16)
    low = (rest - middle.astype(F32)).astype(BF16)
    return jnp.concatenate([high, middle, low], axis=0)


def pick(x, one_hot):
    rows = x.shape[0]
    y = jnp.dot(split(x), one_hot, preferred_element_type=F32)
    return y[:rows] + y[rows : 2 * rows] + y[2 * rows :]


def pack(x, packed):
    if not packed:
        return x
    half, lanes = x.shape[0] // 2, x.shape[1]
    lane = lax.broadcasted_iota(jnp.int32, (half, lanes), 1)
    return jnp.where(lane < lanes // 2, x[:half], pltpu.roll(x[half:], lanes // 2, 1))


def unpack(x, packed):
    if not packed:
        return x
    return jnp.concatenate([x, pltpu.roll(x, x.shape[1] // 2, 1)], axis=0)


def kernel(
    nm, ns,
    x_ref, dep_ref, nb_ref, oe_ref, cnt_ref, ov_ref, er_ref,
    out_ref,
    st, store, halo, dhalo, oh, fc, em, parts, sums,
    h_send, h_recv, d_send, d_recv, e_send, e_recv, f_send, f_recv, s_send, s_recv,
):
    mm, me = lax.axis_index("mem"), lax.axis_index("space")
    lm, _, width = x_ref.shape
    members = nm * lm
    inner = 2 if ns % 2 == 0 else 1
    base = lax.div(me, inner) * inner
    stages = [
        [(mm, base + lax.rem(me - base + d, inner)) for d in range(1, inner)],
        [(mm, lax.rem(me + d * inner, ns)) for d in range(1, ns // inner)],
    ]
    stages = [peers for peers in stages if peers]
    space_peers = sum(stages, []) + [(mm, lax.rem(me + d, ns)) for d in (1, ns - 1)]
    mem_peers = [(lax.rem(mm + d, nm), me) for d in range(1, nm)]

    barrier = pltpu.get_barrier_semaphore()
    for peer in space_peers + mem_peers:
        pl.semaphore_signal(barrier, inc=1, device_id=peer, device_id_type=MESH)

    for n in range(4):
        for f in range(3):
            st[0, f, n] = x_ref[:, f * 4 + n, :]
    has = (me > 0, me < ns - 1)
    for side in range(2):

        @pl.when(jnp.logical_not(has[side]))
        def _():
            for s in range(3):
                halo[s, side] = jnp.zeros(halo.shape[2:], F32)
            dhalo[side] = jnp.zeros(dhalo.shape[1:], F32)

    pl.semaphore_wait(barrier, len(space_peers) + len(mem_peers))

    def halo_copy(s, side):
        first = SENT[1 - side][0]
        target = (mm, lax.rem(me + (ns - 1 if side == 0 else 1), ns))
        return pltpu.make_async_remote_copy(
            src_ref=st.at[s, :, pl.ds(first, 3)],
            dst_ref=halo.at[s, 1 - side],
            send_sem=h_send.at[s, 1 - side],
            recv_sem=h_recv.at[s, 1 - side],
            device_id=target,
            device_id_type=MESH,
        )

    def depth_copy(side):
        target = (mm, lax.rem(me + (ns - 1 if side == 0 else 1), ns))
        return pltpu.make_async_remote_copy(
            src_ref=dep_ref,
            dst_ref=dhalo.at[1 - side],
            send_sem=d_send.at[1 - side],
            recv_sem=d_recv.at[1 - side],
            device_id=target,
            device_id_type=MESH,
        )

    def send_halo(s):
        for side in range(2):

            @pl.when(has[side])
            def _():
                halo_copy(s, side).start()

    for side in range(2):

        @pl.when(has[side])
        def _():
            depth_copy(side).start()

    send_halo(0)

    rows = lax.broadcasted_iota(jnp.int32, (width, width), 0)
    for face in range(4):
        side = FACES[face][4]
        link = nb_ref[face : face + 1, :]
        oh[face, 0] = jnp.where(rows + width == link, 1.0, 0.0).astype(BF16)
        oh[face, 1] = jnp.where(rows + 2 * width * side == link, 1.0, 0.0).astype(BF16)

    slots = ov_ref.shape[1]
    slot = lax.broadcasted_iota(jnp.int32, (1, slots), 1)
    weight = jnp.where(slot < cnt_ref[0], 1.0, 0.0) / er_ref[...]
    square = weight * weight
    both = jnp.concatenate(
        [jnp.broadcast_to(square, (8, slots)), jnp.broadcast_to(square * ov_ref[...], (8, slots))],
        axis=0,
    )
    at = jnp.where(
        lax.broadcasted_iota(jnp.int32, (width, slots), 0) == oe_ref[...], 1.0, 0.0
    ).astype(BF16)
    y = lax.dot_general(split(both), at, (((1,), (1,)), ((), ())), preferred_element_type=F32)
    y = y[:16] + y[16:32] + y[32:]
    w2, wo = y[0:1], y[8:9]

    def tall(ref, n):
        return jnp.broadcast_to(ref[n : n + 1, :], (lm, width))

    own_depth = [tall(dep_ref, n) for n in range(4)]
    depth_out, speed = {}, {}

    for s in range(3):
        q = [[st[s, f, n] for f in range(3)] for n in range(4)]
        near = []
        for face, (_, outer, _, _, side) in enumerate(FACES):
            x = jnp.concatenate([q[n][f] for n in outer for f in range(3)], axis=0)
            near.append(pick(x, oh[face, 0]))
        hu = [own_depth[n] * q[n][1] for n in range(4)]
        hv = [own_depth[n] * q[n][2] for n in range(4)]
        rate = [[None] * 3 for _ in range(4)]
        for n in range(4):
            b, a2 = n % 2, n - n % 2
            rate[n][0] = -((hu[2 + b] - hu[b]) + (hv[a2 + 1] - hv[a2]))
            rate[n][1] = q[b][0] - q[2 + b][0] + CORIOLIS * q[n][2]
            rate[n][2] = q[a2][0] - q[a2 + 1][0] - CORIOLIS * q[n][1]
        if s == 0:
            for side in range(2):

                @pl.when(has[side])
                def _():
                    depth_copy(1 - side).wait_recv()

            for face, (inner, outer, _, _, side) in enumerate(FACES):
                here = jnp.concatenate([own_depth[n] for n in outer], axis=0)
                there = jnp.concatenate([tall(dhalo.at[side], n) for n in outer], axis=0)
                got = pick(here, oh[face, 0]) + pick(there, oh[face, 1])
                for i in range(2):
                    depth_out[face, i] = got[i * lm : (i + 1) * lm]
                    speed[face, i] = jnp.sqrt(
                        jnp.maximum(own_depth[inner[i]], depth_out[face, i])
                    )
        for side in range(2):

            @pl.when(has[side])
            def _():
                halo_copy(s, 1 - side).wait_recv()

        for face, (inner, outer, nx, ny, side) in enumerate(FACES):
            x = jnp.concatenate(
                [halo[s, side, f, SENT[side].index(n)] for n in outer for f in range(3)],
                axis=0,
            )
            far = near[face] + pick(x, oh[face, 1])
            for i in range(2):
                n = inner[i]
                fh, fu, fv = (far[(i * 3 + f) * lm : (i * 3 + f + 1) * lm] for f in range(3))
                sp, do = speed[face, i], depth_out[face, i]
                if nx:
                    rate[n][0] += nx * (hu[n] - do * fu) + sp * (fh - q[n][0])
                    rate[n][1] += nx * (q[n][0] - fh) + sp * (fu - q[n][1])
                    rate[n][2] += sp * (fv - q[n][2])
                else:
                    rate[n][0] += ny * (hv[n] - do * fv) + sp * (fh - q[n][0])
                    rate[n][1] += sp * (fu - q[n][1])
                    rate[n][2] += ny * (q[n][0] - fh) + sp * (fv - q[n][2])
        for n in range(4):
            for f in range(3):
                change = TIME_STEP * rate[n][f]
                if s:
                    change += SECTION_DECAY[s] * store[f, n]
                q[n][f] = q[n][f] + SECTION_GAIN[s] * change
                if s < 2:
                    store[f, n] = change
                    st[s + 1, f, n] = q[n][f]
                else:
                    fc[mm, f, n] = q[n][f]
        if s < 2:
            send_halo(s + 1)

    for f in range(3):
        em[mm, f] = 0.25 * ((q[0][f] + q[1][f]) + (q[2][f] + q[3][f]))

    def share(buf, send, recv, d):
        return pltpu.make_async_remote_copy(
            src_ref=buf.at[mm],
            dst_ref=buf.at[mm],
            send_sem=send.at[d],
            recv_sem=recv.at[d],
            device_id=mem_peers[d],
            device_id_type=MESH,
        )

    em_copies = [share(em, e_send, e_recv, d) for d in range(nm - 1)]
    fc_copies = [share(fc, f_send, f_recv, d) for d in range(nm - 1)]
    for copy in em_copies + fc_copies:
        copy.start()
    for copy in em_copies:
        copy.wait_recv()

    root = math.sqrt(members - 1)
    zs = [jnp.concatenate([em[j, f] for j in range(nm)], axis=0) for f in range(3)]
    zbar = [jnp.sum(z, axis=0, keepdims=True) * (1.0 / members) for z in zs]
    spread = [(z - b) * (1.0 / root) for z, b in zip(zs, zbar)]

    lanes = sums.shape[3]
    packed = sums.shape[2] < members
    row = lax.broadcasted_iota(jnp.int32, (members, lanes), 0)
    lane = lax.broadcasted_iota(jnp.int32, (members, lanes), 1)
    eyes = jnp.where((lane == row) | (lane == row + members), 1.0, 0.0)
    w_row = w_col = None
    sum_copies = []
    for it in range(GN_ITERS):
        c = zbar
        if it:
            c = [
                b + jnp.sum(w_col * z, axis=0, keepdims=True) for b, z in zip(zbar, spread)
            ]
        hx = c[0] + c[1] * c[1] + c[2] * c[2]
        sens = (
            spread[0]
            + spread[1] * (2.0 * c[1] + spread[1])
            + spread[2] * (2.0 * c[2] + spread[2])
        )
        right = jnp.concatenate(
            [
                jnp.zeros((members, width), F32),
                sens * w2,
                jnp.broadcast_to(hx * w2 - wo, (8, width)),
                jnp.zeros((lanes - 2 * members - 8, width), F32),
            ],
            axis=0,
        )
        total = lax.dot_general(
            sens, right, (((1,), (1,)), ((), ())),
            precision=lax.Precision.HIGHEST, preferred_element_type=F32,
        )
        total = pack(total, packed)
        slot_at = 0
        for stage, peers in enumerate(stages):
            sums[it, stage] = total
            copies = [
                pltpu.make_async_remote_copy(
                    src_ref=sums.at[it, stage],
                    dst_ref=parts.at[it, slot_at + d],
                    send_sem=s_send.at[it, slot_at + d],
                    recv_sem=s_recv.at[it, slot_at + d],
                    device_id=peer,
                    device_id_type=MESH,
                )
                for d, peer in enumerate(peers)
            ]
            for copy in copies:
                copy.start()
            for d, copy in enumerate(copies):
                copy.wait_recv()
                total = total + parts[it, slot_at + d]
            slot_at += len(peers)
            sum_copies += copies
        total = unpack(total, packed)
        a = total + eyes
        if it:
            a = a + jnp.where(lane == 2 * members, w_col, 0.0)
        for k in range(members):
            pivot = a[k : k + 1, :]
            col = a[:, members + k : members + k + 1]
            head = col[k : k + 1]
            ratio = pivot * (1.0 / head)
            a = jnp.where(row > k, a - col * ratio, jnp.where(row == k, pivot * lax.rsqrt(head), a))
        step = jnp.sum(a[:, 2 * members : 2 * members + 1] * a, axis=0, keepdims=True)
        w_row = -step if it == 0 else w_row - step
        w_col = jnp.sum(jnp.where(lane == row, w_row, 0.0), axis=1, keepdims=True)

    coef = jnp.where(lane < members, a + w_row * (1.0 / root), 0.0)
    mix = coef + 1.0 / members - jnp.sum(coef, axis=1, keepdims=True) * (1.0 / members)
    own = mix[0:lm]
    for j in range(1, nm):
        own = jnp.where(mm == j, mix[j * lm : (j + 1) * lm], own)
    gains = [jnp.broadcast_to(own[:, m : m + 1], (lm, width)) for m in range(members)]
    for copy in fc_copies:
        copy.wait_recv()
    for n in range(4):
        for f in range(3):
            acc = None
            for j in range(nm):
                block = fc[j, f, n]
                for i in range(lm):
                    term = gains[j * lm + i] * block[i : i + 1, :]
                    acc = term if acc is None else acc + term
            out_ref[f * 4 + n] = acc

    for side in range(2):

        @pl.when(has[side])
        def _():
            depth_copy(side).wait_send()
            for s in range(3):
                halo_copy(s, side).wait_send()

    for copy in em_copies + fc_copies + sum_copies:
        copy.wait_send()


def solution(mesh):
    nm, ns = mesh.shape["mem"], mesh.shape["space"]

    def body(states, depth, neighbours, obs_element, obs_count, obs_values, obs_error):
        lm, comps, width = states.shape
        slots = obs_values.shape[0]
        members = nm * lm
        lanes = -(-(2 * members + 8) // 128) * 128
        packed = members % 16 == 0 and 4 * members + 2 <= lanes
        rows = members // 2 if packed else members
        vmem = pl.BlockSpec(memory_space=pltpu.VMEM)
        dma = pltpu.SemaphoreType.DMA
        peers = max(nm - 1, 1)
        mixed = pl.pallas_call(
            functools.partial(kernel, nm, ns),
            out_shape=jax.ShapeDtypeStruct((comps, lm, width), F32),
            in_specs=[vmem] * 4 + [pl.BlockSpec(memory_space=pltpu.SMEM)] + [vmem] * 2,
            out_specs=vmem,
            scratch_shapes=[
                pltpu.VMEM((3, 3, 4, lm, width), F32),
                pltpu.VMEM((3, 4, lm, width), F32),
                pltpu.VMEM((3, 2, 3, 3, lm, width), F32),
                pltpu.VMEM((2, 4, width), F32),
                pltpu.VMEM((4, 2, width, width), BF16),
                pltpu.VMEM((nm, 3, 4, lm, width), F32),
                pltpu.VMEM((nm, 3, lm, width), F32),
                pltpu.VMEM((GN_ITERS, ns - 1, rows, lanes), F32),
                pltpu.VMEM((GN_ITERS, 2, rows, lanes), F32),
                dma((3, 2)),
                dma((3, 2)),
                dma((2,)),
                dma((2,)),
                dma((peers,)),
                dma((peers,)),
                dma((peers,)),
                dma((peers,)),
                dma((GN_ITERS, ns - 1)),
                dma((GN_ITERS, ns - 1)),
            ],
            compiler_params=pltpu.CompilerParams(
                collective_id=0, has_side_effects=True, vmem_limit_bytes=40 * 1024 * 1024
            ),
        )(
            states,
            depth,
            neighbours,
            obs_element.reshape(1, slots),
            obs_count,
            obs_values.reshape(1, slots),
            obs_error.reshape(1, slots),
        )
        return mixed.transpose(1, 0, 2)

    placed = (
        P("mem", None, "space"),
        P(None, "space"),
        P(None, "space"),
        P("space"),
        P("space"),
        P("space"),
        P("space"),
    )
    return jax.shard_map(
        body, mesh=mesh, in_specs=placed, out_specs=P("mem", None, "space"), check_vma=False
    )
```

```python
import functools
import math

import jax
import jax.numpy as jnp
from jax import lax
from jax.experimental import pallas as pl
from jax.experimental.pallas import tpu as pltpu
from jax.sharding import PartitionSpec as P

GN_ITERS = 2
CORIOLIS = 0.5
TIME_STEP = 0.08
SECTION_DECAY = (0.0, -5.0 / 9.0, -153.0 / 128.0)
SECTION_GAIN = (1.0 / 3.0, 15.0 / 16.0, 8.0 / 15.0)
FACES = (
    ((0, 1), (2, 3), -1.0, 0.0, 0),
    ((2, 3), (0, 1), 1.0, 0.0, 1),
    ((0, 2), (1, 3), 0.0, -1.0, 0),
    ((1, 3), (0, 2), 0.0, 1.0, 1),
)
SENT = ((1, 2, 3), (0, 1, 2))
MESH = pl.DeviceIdType.MESH
F32, BF16 = jnp.float32, jnp.bfloat16


def split(x):
    high = x.astype(BF16)
    rest = x - high.astype(F32)
    middle = rest.astype(BF16)
    low = (rest - middle.astype(F32)).astype(BF16)
    return jnp.concatenate([high, middle, low], axis=0)


def pick(x, one_hot):
    rows = x.shape[0]
    y = jnp.dot(split(x), one_hot, preferred_element_type=F32)
    return y[:rows] + y[rows : 2 * rows] + y[2 * rows :]


def pack(x, packed):
    if not packed:
        return x
    half, lanes = x.shape[0] // 2, x.shape[1]
    lane = lax.broadcasted_iota(jnp.int32, (half, lanes), 1)
    return jnp.where(lane < lanes // 2, x[:half], pltpu.roll(x[half:], lanes // 2, 1))


def unpack(x, packed):
    if not packed:
        return x
    return jnp.concatenate([x, pltpu.roll(x, x.shape[1] // 2, 1)], axis=0)


def kernel(
    nm, ns,
    x_ref, dep_ref, nb_ref, oe_ref, cnt_ref, ov_ref, er_ref,
    out_ref,
    st, store, halo, dhalo, oh, fc, em, parts, sums,
    h_send, h_recv, d_send, d_recv, e_send, e_recv, f_send, f_recv, s_send, s_recv,
):
    mm, me = lax.axis_index("mem"), lax.axis_index("space")
    lm, _, width = x_ref.shape
    members = nm * lm
    inner = 2 if ns % 2 == 0 else 1
    base = lax.div(me, inner) * inner
    stages = [
        [(mm, base + lax.rem(me - base + d, inner)) for d in range(1, inner)],
        [(mm, lax.rem(me + d * inner, ns)) for d in range(1, ns // inner)],
    ]
    stages = [peers for peers in stages if peers]
    space_peers = sum(stages, []) + [(mm, lax.rem(me + d, ns)) for d in (1, ns - 1)]
    mem_peers = [(lax.rem(mm + d, nm), me) for d in range(1, nm)]

    barrier = pltpu.get_barrier_semaphore()
    for peer in space_peers + mem_peers:
        pl.semaphore_signal(barrier, inc=1, device_id=peer, device_id_type=MESH)

    for n in range(4):
        for f in range(3):
            st[0, f, n] = x_ref[:, f * 4 + n, :]
    has = (me > 0, me < ns - 1)
    for side in range(2):

        @pl.when(jnp.logical_not(has[side]))
        def _():
            for s in range(3):
                halo[s, side] = jnp.zeros(halo.shape[2:], F32)
            dhalo[side] = jnp.zeros(dhalo.shape[1:], F32)

    pl.semaphore_wait(barrier, len(space_peers) + len(mem_peers))

    def halo_copy(s, side):
        first = SENT[1 - side][0]
        target = (mm, lax.rem(me + (ns - 1 if side == 0 else 1), ns))
        return pltpu.make_async_remote_copy(
            src_ref=st.at[s, :, pl.ds(first, 3)],
            dst_ref=halo.at[s, 1 - side],
            send_sem=h_send.at[s, 1 - side],
            recv_sem=h_recv.at[s, 1 - side],
            device_id=target,
            device_id_type=MESH,
        )

    def depth_copy(side):
        target = (mm, lax.rem(me + (ns - 1 if side == 0 else 1), ns))
        return pltpu.make_async_remote_copy(
            src_ref=dep_ref,
            dst_ref=dhalo.at[1 - side],
            send_sem=d_send.at[1 - side],
            recv_sem=d_recv.at[1 - side],
            device_id=target,
            device_id_type=MESH,
        )

    def send_halo(s):
        for side in range(2):

            @pl.when(has[side])
            def _():
                halo_copy(s, side).start()

    for side in range(2):

        @pl.when(has[side])
        def _():
            depth_copy(side).start()

    send_halo(0)

    rows = lax.broadcasted_iota(jnp.int32, (width, width), 0)
    for face in range(4):
        side = FACES[face][4]
        link = nb_ref[face : face + 1, :]
        oh[face, 0] = jnp.where(rows + width == link, 1.0, 0.0).astype(BF16)
        oh[face, 1] = jnp.where(rows + 2 * width * side == link, 1.0, 0.0).astype(BF16)

    slots = ov_ref.shape[1]
    slot = lax.broadcasted_iota(jnp.int32, (1, slots), 1)
    weight = jnp.where(slot < cnt_ref[0], 1.0, 0.0) / er_ref[...]
    square = weight * weight
    both = jnp.concatenate(
        [jnp.broadcast_to(square, (8, slots)), jnp.broadcast_to(square * ov_ref[...], (8, slots))],
        axis=0,
    )
    at = jnp.where(
        lax.broadcasted_iota(jnp.int32, (width, slots), 0) == oe_ref[...], 1.0, 0.0
    ).astype(BF16)
    y = lax.dot_general(split(both), at, (((1,), (1,)), ((), ())), preferred_element_type=F32)
    y = y[:16] + y[16:32] + y[32:]
    w2, wo = y[0:1], y[8:9]

    def tall(ref, n):
        return jnp.broadcast_to(ref[n : n + 1, :], (lm, width))

    own_depth = [tall(dep_ref, n) for n in range(4)]
    depth_out, speed = {}, {}

    for s in range(3):
        q = [[st[s, f, n] for f in range(3)] for n in range(4)]
        near = []
        for face, (_, outer, _, _, side) in enumerate(FACES):
            x = jnp.concatenate([q[n][f] for n in outer for f in range(3)], axis=0)
            near.append(pick(x, oh[face, 0]))
        hu = [own_depth[n] * q[n][1] for n in range(4)]
        hv = [own_depth[n] * q[n][2] for n in range(4)]
        rate = [[None] * 3 for _ in range(4)]
        for n in range(4):
            b, a2 = n % 2, n - n % 2
            rate[n][0] = -((hu[2 + b] - hu[b]) + (hv[a2 + 1] - hv[a2]))
            rate[n][1] = q[b][0] - q[2 + b][0] + CORIOLIS * q[n][2]
            rate[n][2] = q[a2][0] - q[a2 + 1][0] - CORIOLIS * q[n][1]
        if s == 0:
            for side in range(2):

                @pl.when(has[side])
                def _():
                    depth_copy(1 - side).wait_recv()

            for face, (inner, outer, _, _, side) in enumerate(FACES):
                here = jnp.concatenate([own_depth[n] for n in outer], axis=0)
                there = jnp.concatenate([tall(dhalo.at[side], n) for n in outer], axis=0)
                got = pick(here, oh[face, 0]) + pick(there, oh[face, 1])
                for i in range(2):
                    depth_out[face, i] = got[i * lm : (i + 1) * lm]
                    speed[face, i] = jnp.sqrt(
                        jnp.maximum(own_depth[inner[i]], depth_out[face, i])
                    )
        waited = set()
        for face in (0, 2, 1, 3):
            inner, outer, nx, ny, side = FACES[face]
            if side not in waited:
                waited.add(side)

                @pl.when(has[side])
                def _():
                    halo_copy(s, 1 - side).wait_recv()

            x = jnp.concatenate(
                [halo[s, side, f, SENT[side].index(n)] for n in outer for f in range(3)],
                axis=0,
            )
            far = near[face] + pick(x, oh[face, 1])
            for i in range(2):
                n = inner[i]
                fh, fu, fv = (far[(i * 3 + f) * lm : (i * 3 + f + 1) * lm] for f in range(3))
                sp, do = speed[face, i], depth_out[face, i]
                if nx:
                    rate[n][0] += nx * (hu[n] - do * fu) + sp * (fh - q[n][0])
                    rate[n][1] += nx * (q[n][0] - fh) + sp * (fu - q[n][1])
                    rate[n][2] += sp * (fv - q[n][2])
                else:
                    rate[n][0] += ny * (hv[n] - do * fv) + sp * (fh - q[n][0])
                    rate[n][1] += sp * (fu - q[n][1])
                    rate[n][2] += ny * (q[n][0] - fh) + sp * (fv - q[n][2])
        for n in range(4):
            for f in range(3):
                change = TIME_STEP * rate[n][f]
                if s:
                    change += SECTION_DECAY[s] * store[f, n]
                q[n][f] = q[n][f] + SECTION_GAIN[s] * change
                if s < 2:
                    store[f, n] = change
                    st[s + 1, f, n] = q[n][f]
                else:
                    fc[mm, f, n] = q[n][f]
        if s < 2:
            send_halo(s + 1)

    for f in range(3):
        em[mm, f] = 0.25 * ((q[0][f] + q[1][f]) + (q[2][f] + q[3][f]))

    def share(buf, send, recv, d):
        return pltpu.make_async_remote_copy(
            src_ref=buf.at[mm],
            dst_ref=buf.at[mm],
            send_sem=send.at[d],
            recv_sem=recv.at[d],
            device_id=mem_peers[d],
            device_id_type=MESH,
        )

    em_copies = [share(em, e_send, e_recv, d) for d in range(nm - 1)]
    fc_copies = [share(fc, f_send, f_recv, d) for d in range(nm - 1)]
    for copy in em_copies + fc_copies:
        copy.start()
    for copy in em_copies:
        copy.wait_recv()

    root = math.sqrt(members - 1)
    zs = [jnp.concatenate([em[j, f] for j in range(nm)], axis=0) for f in range(3)]
    zbar = [jnp.sum(z, axis=0, keepdims=True) * (1.0 / members) for z in zs]
    spread = [(z - b) * (1.0 / root) for z, b in zip(zs, zbar)]

    lanes = sums.shape[3]
    packed = sums.shape[2] < members
    row = lax.broadcasted_iota(jnp.int32, (members, lanes), 0)
    lane = lax.broadcasted_iota(jnp.int32, (members, lanes), 1)
    eyes = jnp.where((lane == row) | (lane == row + members), 1.0, 0.0)
    w_row = w_col = None
    sum_copies = []
    for it in range(GN_ITERS):
        c = zbar
        if it:
            c = [
                b + jnp.sum(w_col * z, axis=0, keepdims=True) for b, z in zip(zbar, spread)
            ]
        hx = c[0] + c[1] * c[1] + c[2] * c[2]
        sens = (
            spread[0]
            + spread[1] * (2.0 * c[1] + spread[1])
            + spread[2] * (2.0 * c[2] + spread[2])
        )
        right = jnp.concatenate(
            [
                jnp.zeros((members, width), F32),
                sens * w2,
                jnp.broadcast_to(hx * w2 - wo, (8, width)),
                jnp.zeros((lanes - 2 * members - 8, width), F32),
            ],
            axis=0,
        )
        total = lax.dot_general(
            sens, right, (((1,), (1,)), ((), ())),
            precision=lax.Precision.HIGHEST, preferred_element_type=F32,
        )
        total = pack(total, packed)
        slot_at = 0
        for stage, peers in enumerate(stages):
            sums[it, stage] = total
            copies = [
                pltpu.make_async_remote_copy(
                    src_ref=sums.at[it, stage],
                    dst_ref=parts.at[it, slot_at + d],
                    send_sem=s_send.at[it, slot_at + d],
                    recv_sem=s_recv.at[it, slot_at + d],
                    device_id=peer,
                    device_id_type=MESH,
                )
                for d, peer in enumerate(peers)
            ]
            for copy in copies:
                copy.start()
            for d, copy in enumerate(copies):
                copy.wait_recv()
                total = total + parts[it, slot_at + d]
            slot_at += len(peers)
            sum_copies += copies
        total = unpack(total, packed)
        a = total + eyes
        if it:
            a = a + jnp.where(lane == 2 * members, w_col, 0.0)
        for k in range(members):
            pivot = a[k : k + 1, :]
            col = a[:, members + k : members + k + 1]
            head = col[k : k + 1]
            ratio = pivot * (1.0 / head)
            a = jnp.where(row > k, a - col * ratio, jnp.where(row == k, pivot * lax.rsqrt(head), a))
        step = jnp.sum(a[:, 2 * members : 2 * members + 1] * a, axis=0, keepdims=True)
        w_row = -step if it == 0 else w_row - step
        w_col = jnp.sum(jnp.where(lane == row, w_row, 0.0), axis=1, keepdims=True)

    coef = jnp.where(lane < members, a + w_row * (1.0 / root), 0.0)
    mix = coef + 1.0 / members - jnp.sum(coef, axis=1, keepdims=True) * (1.0 / members)
    own = mix[0:lm]
    for j in range(1, nm):
        own = jnp.where(mm == j, mix[j * lm : (j + 1) * lm], own)
    gains = [jnp.broadcast_to(own[:, m : m + 1], (lm, width)) for m in range(members)]
    for copy in fc_copies:
        copy.wait_recv()
    for n in range(4):
        for f in range(3):
            acc = None
            for j in range(nm):
                block = fc[j, f, n]
                for i in range(lm):
                    term = gains[j * lm + i] * block[i : i + 1, :]
                    acc = term if acc is None else acc + term
            out_ref[f * 4 + n] = acc

    for side in range(2):

        @pl.when(has[side])
        def _():
            depth_copy(side).wait_send()
            for s in range(3):
                halo_copy(s, side).wait_send()

    for copy in em_copies + fc_copies + sum_copies:
        copy.wait_send()


def solution(mesh):
    nm, ns = mesh.shape["mem"], mesh.shape["space"]

    def body(states, depth, neighbours, obs_element, obs_count, obs_values, obs_error):
        lm, comps, width = states.shape
        slots = obs_values.shape[0]
        members = nm * lm
        lanes = -(-(2 * members + 8) // 128) * 128
        packed = members % 16 == 0 and 4 * members + 2 <= lanes
        rows = members // 2 if packed else members
        vmem = pl.BlockSpec(memory_space=pltpu.VMEM)
        dma = pltpu.SemaphoreType.DMA
        peers = max(nm - 1, 1)
        mixed = pl.pallas_call(
            functools.partial(kernel, nm, ns),
            out_shape=jax.ShapeDtypeStruct((comps, lm, width), F32),
            in_specs=[vmem] * 4 + [pl.BlockSpec(memory_space=pltpu.SMEM)] + [vmem] * 2,
            out_specs=vmem,
            scratch_shapes=[
                pltpu.VMEM((3, 3, 4, lm, width), F32),
                pltpu.VMEM((3, 4, lm, width), F32),
                pltpu.VMEM((3, 2, 3, 3, lm, width), F32),
                pltpu.VMEM((2, 4, width), F32),
                pltpu.VMEM((4, 2, width, width), BF16),
                pltpu.VMEM((nm, 3, 4, lm, width), F32),
                pltpu.VMEM((nm, 3, lm, width), F32),
                pltpu.VMEM((GN_ITERS, ns - 1, rows, lanes), F32),
                pltpu.VMEM((GN_ITERS, 2, rows, lanes), F32),
                dma((3, 2)),
                dma((3, 2)),
                dma((2,)),
                dma((2,)),
                dma((peers,)),
                dma((peers,)),
                dma((peers,)),
                dma((peers,)),
                dma((GN_ITERS, ns - 1)),
                dma((GN_ITERS, ns - 1)),
            ],
            compiler_params=pltpu.CompilerParams(
                collective_id=0, has_side_effects=True, vmem_limit_bytes=40 * 1024 * 1024
            ),
        )(
            states,
            depth,
            neighbours,
            obs_element.reshape(1, slots),
            obs_count,
            obs_values.reshape(1, slots),
            obs_error.reshape(1, slots),
        )
        return mixed.transpose(1, 0, 2)

    placed = (
        P("mem", None, "space"),
        P(None, "space"),
        P(None, "space"),
        P("space"),
        P("space"),
        P("space"),
        P("space"),
    )
    return jax.shard_map(
        body, mesh=mesh, in_specs=placed, out_specs=P("mem", None, "space"), check_vma=False
    )
```
